32 devices in a mesh: node: 8 (over y, x, core), fld: 4 (over z).
Axes of the slice: x: 2, y: 2, z: 4, core: 2. Of those that a mesh axis runs over, the one named last changes fastest.
Arguments:
- pressure: bfloat16 [57344, 128], P(('node', 'fld')), may hold values from -6 to 6
- modes: bfloat16 [57344, 2816], P(('node', 'fld')), may hold values from -0.0234375 to 0.0234375
- omega_mode: float32 [2816], replicated, may hold values from 0.5 to 4
- damping: float32 [2816], replicated, may hold values from 0.02 to 0.2
- omega_force: float32 [8], replicated, may hold values from 0.8 to 3
- panel_of: int32 [57344], P(('node', 'fld')), may hold values from 0 to 255
- dist_bin: int32 [8192, 256], P('node', 'fld'), may hold values from 0 to 399
Outputs:
- field_pressure: float32 [256, 128], P('fld')
The draws below stay inside these ranges and needn't reach their ends.
All inputs are finite; a program needn't handle non-finite values.
Results may differ from the reference program's by a relative error of at most 0.0031.
Values may be sent and summed in bfloat16 or wider, within the bound.
No kernel may reach another device: no remote copies, remote signals or barrier semaphores. Data moves between devices by JAX's collectives and lax.ppermute only.
A program may use at most 64 MiB of HBM per device.

```python
import math
import jax
import jax.numpy as jnp
from jax import lax

MODES = 2816
FREQS = 8
REALIZ = 8
FIELD = 256
NODE_DEV = 1792
PANEL_DEV = 256
NODES = 57344
PANELS = 8192


def place_ends(entries, stream_key, least, largest):
    extent = entries.shape
    place = [jax.random.randint(jax.random.fold_in(stream_key, axis), (), 0, extent[axis]) for axis in range(len(extent))]
    entries = entries.at[tuple(place)].set(least)
    longest = extent.index(max(extent))
    place[longest] = (place[longest] + 1) % extent[longest]
    return entries.at[tuple(place)].set(largest)


def steps_of(rng, shape, cuts, least, high):
    factor_of, own = 1.0, jax.random.fold_in(rng, 6)
    for axis_at, blocks in cuts:
        heights = jnp.exp(jax.random.uniform(jax.random.fold_in(own, axis_at), (blocks,), jnp.float32, least / len(cuts), high / len(cuts)))
        factor_of = factor_of * jnp.repeat(heights, shape[axis_at] // blocks).reshape([-1 if axis == axis_at else 1 for axis in range(len(shape))])
    return factor_of


def noise(rng, extent, deviation, limit, split=(), kind=jnp.bfloat16):
    level = steps_of(rng, extent, split, -0.22, 0.18) if split else 1.0
    drawn = jax.random.normal(rng, extent, jnp.float32) * deviation * level
    return jnp.minimum(jnp.maximum(drawn, -limit), limit).astype(kind)


def setup_inputs(seed: int = 0) -> dict:
    keys = jax.random.split(jax.random.key(seed), 8)
    pressure = noise(keys[0], (NODES, 2 * FREQS * REALIZ), 1.0, 6.0, ((0, 32),))
    modes = noise(keys[1], (NODES, MODES), NODES ** -0.5, 0.0234375, ((0, 32),))
    omega_mode = jnp.clip(jnp.exp(jax.random.uniform(keys[2], (MODES,), jnp.float32, math.log(0.5), math.log(4.0))), 0.5, 4.0)
    damping = jnp.clip(jnp.exp(jax.random.uniform(keys[3], (MODES,), jnp.float32, math.log(0.02), math.log(0.2))), 0.02, 0.2)
    omega_force = jnp.clip(jax.random.uniform(keys[4], (FREQS,), jnp.float32, 0.8, 3.0), 0.8, 3.0)
    panel_of = place_ends(jax.random.randint(keys[5], (NODES,), 0, PANEL_DEV), jax.random.fold_in(keys[5], 1), 0, PANEL_DEV - 1).astype(jnp.int32)
    dist_bin = place_ends(jax.random.randint(keys[6], (PANELS, FIELD), 0, 400), jax.random.fold_in(keys[6], 1), 0, 399).astype(jnp.int32)
    return {"pressure": pressure, "modes": modes, "omega_mode": omega_mode, "damping": damping, "omega_force": omega_force, "panel_of": panel_of, "dist_bin": dist_bin}


def modal_response(forces, omega_mode, damping, omega_force):
    half = forces.shape[1] // 2
    wcol = jnp.repeat(omega_force, half // omega_force.shape[0])[None, :]
    wmod = omega_mode[:, None]
    real_part = wmod * wmod - wcol * wcol
    imag_part = 2.0 * damping[:, None] * wmod * wcol
    magnitude = real_part * real_part + imag_part * imag_part
    h_real = real_part / magnitude
    h_imag = -imag_part / magnitude
    f_real = forces[:, :half]
    f_imag = forces[:, half:]
    a_real = h_real * f_real - h_imag * f_imag
    a_imag = h_real * f_imag + h_imag * f_real
    return jnp.concatenate([a_real, a_imag], axis=1).astype(jnp.bfloat16)


def reference(pressure, modes, omega_mode, damping, omega_force, panel_of, dist_bin):
    forces = lax.dot_general(modes, pressure, (((0,), (0,)), ((), ())), preferred_element_type=jnp.float32)
    response = modal_response(forces, omega_mode, damping, omega_force)
    raw = jnp.dot(modes, response, preferred_element_type=jnp.float32)
    half = raw.shape[1] // 2
    wcol = jnp.repeat(omega_force, half // FREQS)[None, :]
    velocity = jnp.concatenate([-wcol * raw[:, half:], wcol * raw[:, :half]], axis=1)
    slab = (jnp.arange(NODES, dtype=jnp.int32) // NODE_DEV).astype(jnp.int32)
    panel_ids = (slab * PANEL_DEV + panel_of).astype(jnp.int32)
    panel_velocity = jax.ops.segment_sum(velocity, panel_ids, num_segments=PANELS)
    shaped = panel_velocity.reshape(PANELS, 2, FREQS, REALIZ)
    dist = 1.0 + 0.05 * dist_bin.astype(jnp.float32)
    outs_real = []
    outs_imag = []
    for freq in range(FREQS):
        omega = omega_force[freq]
        amplitude = 0.01 * omega / (2.0 * jnp.pi * dist)
        k_real = amplitude * jnp.sin(omega * dist)
        k_imag = amplitude * jnp.cos(omega * dist)
        u_real = shaped[:, 0, freq, :]
        u_imag = shaped[:, 1, freq, :]
        hp = lax.Precision.HIGHEST
        p_real = jnp.dot(k_real.T, u_real, precision=hp) - jnp.dot(k_imag.T, u_imag, precision=hp)
        p_imag = jnp.dot(k_real.T, u_imag, precision=hp) + jnp.dot(k_imag.T, u_real, precision=hp)
        outs_real.append(p_real)
        outs_imag.append(p_imag)
    total = jnp.stack([jnp.stack(outs_real, axis=1), jnp.stack(outs_imag, axis=1)], axis=1)
    return total.reshape(FIELD, 2 * FREQS * REALIZ)
```

```python
import math

import jax
import jax.numpy as jnp
from jax import lax
from jax.experimental import pallas as pl
from jax.experimental.pallas import tpu as pltpu
from jax.sharding import PartitionSpec as P

PANEL_DEV = 256
BF16, F16, F32 = jnp.bfloat16, jnp.float16, jnp.float32
NT = (((1,), (1,)), ((), ()))
MIB = 1024 * 1024


def row_block(rows):
    return next(b for b in (256, 128, 64, 32, 16, rows) if rows % b == 0)


def forces_kernel(half_ref, pressure_ref, modes_ref, out_ref, top_ref):
    step = pl.program_id(0)
    part = lax.dot_general(
        pressure_ref[...], modes_ref[...], (((0,), (0,)), ((), ())), preferred_element_type=F32
    )

    @pl.when(step == 0)
    def _():
        out_ref[...] = part

    @pl.when(step > 0)
    def _():
        out_ref[...] += part

    @pl.when(step == pl.num_programs(0) - 1)
    def _():
        top_ref[...] = jnp.full(top_ref.shape, jnp.max(jnp.abs(out_ref[...])), F32)


def forces_half(half, pressure, modes):
    nodes, columns = pressure.shape
    width = modes.shape[1] // 2
    rows = row_block(nodes)
    return pl.pallas_call(
        forces_kernel,
        grid_spec=pltpu.PrefetchScalarGridSpec(
            num_scalar_prefetch=1,
            grid=(nodes // rows,),
            in_specs=[
                pl.BlockSpec((rows, columns), lambda k, h: (k, 0)),
                pl.BlockSpec((rows, width), lambda k, h: (k, h[0])),
            ],
            out_specs=[
                pl.BlockSpec((columns, width), lambda k, h: (0, 0)),
                pl.BlockSpec((8, 128), lambda k, h: (0, 0)),
            ],
        ),
        out_shape=[
            jax.ShapeDtypeStruct((columns, width), F32),
            jax.ShapeDtypeStruct((8, 128), F32),
        ],
        compiler_params=pltpu.CompilerParams(vmem_limit_bytes=16 * MIB),
        cost_estimate=pl.CostEstimate(
            flops=2 * nodes * columns * width, bytes_accessed=2 * nodes * width, transcendentals=0
        ),
        name="forces_half",
    )(half, pressure, modes)


def panel_modes_kernel(panel_ref, modes_ref, high_ref, low_ref, onehot_ref):
    @pl.when(pl.program_id(0) == 0)
    def _():
        panels = lax.broadcasted_iota(jnp.int32, onehot_ref.shape, 0)
        onehot_ref[...] = jnp.where(panels == panel_ref[...], 1.0, 0.0).astype(BF16)

    total = jnp.dot(onehot_ref[...], modes_ref[...], preferred_element_type=F32)
    high = total.astype(BF16)
    high_ref[...] = high
    low_ref[...] = (total - high.astype(F32)).astype(BF16)


def panel_modes(panel_of, modes):
    nodes, count = modes.shape
    width = 256
    return pl.pallas_call(
        panel_modes_kernel,
        grid=(count // width,),
        in_specs=[
            pl.BlockSpec((1, nodes), lambda j: (0, 0)),
            pl.BlockSpec((nodes, width), lambda j: (0, j)),
        ],
        out_specs=[pl.BlockSpec((PANEL_DEV, width), lambda j: (0, j))] * 2,
        out_shape=[jax.ShapeDtypeStruct((PANEL_DEV, count), BF16)] * 2,
        scratch_shapes=[pltpu.VMEM((PANEL_DEV, nodes), BF16)],
        compiler_params=pltpu.CompilerParams(vmem_limit_bytes=16 * MIB),
        cost_estimate=pl.CostEstimate(
            flops=2 * nodes * PANEL_DEV * count, bytes_accessed=2 * nodes * count, transcendentals=0
        ),
        name="panel_modes",
    )(panel_of.reshape(1, nodes), modes)


def sin_cos(angle):
    turns = jnp.floor(angle * (2.0 / math.pi) + 0.5)
    rest = angle - turns * 1.5703125
    rest = rest - turns * 4.837512969970703125e-4
    rest = rest - turns * 7.549789948768648e-8
    square = rest * rest
    sine = rest + rest * square * (
        -1.6666654611e-1 + square * (8.3321608736e-3 - square * 1.9515295891e-4)
    )
    cosine = (1.0 - 0.5 * square) + square * square * (
        4.166664568298827e-2 + square * (-1.388731625493765e-3 + square * 2.443315711809948e-5)
    )
    quadrant = turns.astype(jnp.int32)
    swap = (quadrant & 1) == 1
    sin_sign = jnp.where((quadrant & 2) == 2, -1.0, 1.0)
    cos_sign = jnp.where(((quadrant + 1) & 2) == 2, -1.0, 1.0)
    return jnp.where(swap, cosine, sine) * sin_sign, jnp.where(swap, sine, cosine) * cos_sign


def radiation_kernel(omega_ref, bins_ref, high_ref, low_ref):
    omega = omega_ref[pl.program_id(0)]
    dist = 1.0 + 0.05 * bins_ref[...].astype(F32)
    sine, cosine = sin_cos(omega * dist)
    gain = (-0.01 / (2.0 * math.pi)) * omega * omega / dist
    for part, value in enumerate((gain * cosine, -gain * sine)):
        high = value.astype(BF16)
        high_ref[part, 0] = high
        low_ref[part, 0] = (value - high.astype(F32)).astype(BF16)


def radiation(omega_force, bins):
    field, panels = bins.shape
    freqs = omega_force.shape[0]
    return pl.pallas_call(
        radiation_kernel,
        grid=(freqs,),
        in_specs=[
            pl.BlockSpec(memory_space=pltpu.SMEM),
            pl.BlockSpec((field, panels), lambda f: (0, 0)),
        ],
        out_specs=[pl.BlockSpec((2, 1, field, panels), lambda f: (0, f, 0, 0))] * 2,
        out_shape=[jax.ShapeDtypeStruct((2, freqs, field, panels), BF16)] * 2,
        compiler_params=pltpu.CompilerParams(vmem_limit_bytes=16 * MIB),
        cost_estimate=pl.CostEstimate(
            flops=40 * freqs * field * panels, bytes_accessed=4 * freqs * field * panels, transcendentals=0
        ),
        name="radiation",
    )(omega_force, bins)


def panel_sums_kernel(place_ref, *refs):
    *slots, high_ref, low_ref, out_ref, held_ref = refs
    core, chip = place_ref[0], place_ref[1]
    count = len(slots) // 2
    group = slots[0].shape[1]
    half = held_ref.shape[1] // 2
    width = held_ref.shape[2]
    if count == 1:
        for side in range(2):
            held_ref[side] = slots[side][...].reshape(2 * half, width)
    else:
        for side in range(2):
            for k in range(count):
                start = pl.multiple_of((chip ^ k) * group, group)
                for part in range(2):
                    held_ref[side, pl.ds(part * half + start, group), :] = slots[side * count + k][part]
    total = None
    for side in range(2):
        columns = pl.ds(pl.multiple_of((core ^ side) * width, 128), width)
        for ref in (high_ref, low_ref):
            term = lax.dot_general(held_ref[side], ref[:, columns], NT, preferred_element_type=F32)
            total = term if total is None else total + term
    out_ref[...] = total.astype(out_ref.dtype)


def panel_sums(place, slots, high, low):
    half = slots[0].shape[1] * (len(slots) // 2)
    width = slots[0].shape[2]
    vmem = pl.BlockSpec(memory_space=pltpu.VMEM)
    return pl.pallas_call(
        panel_sums_kernel,
        in_specs=[pl.BlockSpec(memory_space=pltpu.SMEM)] + [vmem] * (len(slots) + 2),
        out_specs=vmem,
        out_shape=jax.ShapeDtypeStruct((2 * half, PANEL_DEV), BF16),
        scratch_shapes=[pltpu.VMEM((2, 2 * half, width), BF16)],
        compiler_params=pltpu.CompilerParams(vmem_limit_bytes=16 * MIB),
        name="panel_sums",
    )(place, *slots, high, low)


def field_kernel(place_ref, *refs):
    *pieces, high_ref, low_ref, out_ref = refs
    parts, freqs, field, panels = high_ref.shape
    own = place_ref[2]
    total = [None, None]
    for k, piece in enumerate(pieces):
        columns = pl.ds(pl.multiple_of((own ^ k) * PANEL_DEV, PANEL_DEV), PANEL_DEV)
        for part in range(2):
            for ref in (high_ref, low_ref):
                left = ref[part, :, :, columns].reshape(freqs * field, PANEL_DEV)
                term = lax.dot_general(left, piece[...], NT, preferred_element_type=F32)
                total[part] = term if total[part] is None else total[part] + term
    columns = out_ref.shape[1]
    half = columns // 2
    column = lax.broadcasted_iota(jnp.int32, (field, columns), 1)
    freq_of = (column % half) // (half // freqs)
    sums = []
    for part in range(2):
        shaped = total[part].reshape(freqs, field, columns)
        picked = jnp.zeros((field, columns), F32)
        for f in range(freqs):
            picked = jnp.where(freq_of == f, shaped[f], picked)
        sums.append(picked)
    turned = pltpu.roll(sums[1], half, 1)
    out_ref[...] = sums[0] + jnp.where(column < half, -turned, turned)


def field_sums(place, pieces, high, low):
    parts, freqs, field, panels = high.shape
    columns = pieces[0].shape[0]
    vmem = pl.BlockSpec(memory_space=pltpu.VMEM)
    return pl.pallas_call(
        field_kernel,
        in_specs=[pl.BlockSpec(memory_space=pltpu.SMEM)] + [vmem] * (len(pieces) + 2),
        out_specs=vmem,
        out_shape=jax.ShapeDtypeStruct((field, columns), F32),
        compiler_params=pltpu.CompilerParams(vmem_limit_bytes=24 * MIB),
        name="field_sums",
    )(place, *pieces, high, low)


def tree(terms):
    while len(terms) > 1:
        terms = [a + b for a, b in zip(terms[::2], terms[1::2], strict=True)]
    return terms[0]


def swap(x, axis, size, k):
    return lax.ppermute(x, axis, [(i, i ^ k) for i in range(size)])


def pack(x, shift):
    scaled = (x * jnp.exp2(shift)).astype(F16)
    note = jnp.broadcast_to(shift.astype(F16), (*x.shape[:-1], 128))
    return jnp.concatenate([scaled, note], axis=-1)


def unpack(y):
    shift = y[(0,) * (y.ndim - 1) + (-1,)].astype(F32)
    return y[..., :-128].astype(F32) * jnp.exp2(-shift), shift


def shards(nodes_axis, field_axis):
    chips = nodes_axis // 2
    chip_bits = chips.bit_length() - 1

    def body(pressure, modes, omega_mode, damping, omega_force, panel_of, dist_bin):
        columns = pressure.shape[1]
        half = columns // 2
        width = modes.shape[1] // 2
        group = half // chips
        node = lax.axis_index("node")
        core, chip, fld = node % 2, node // 2, lax.axis_index("fld")
        place = jnp.stack([core, chip, fld]).astype(jnp.int32)

        away, away_top = forces_half((1 - core).reshape(1), pressure, modes)
        came, came_top = (swap(x, "node", nodes_axis, 1) for x in (away, away_top))
        home, home_top = forces_half(core.reshape(1), pressure, modes)
        total = (home + came).reshape(2, half, width)
        bound = jnp.maximum(home_top[0, 0] + came_top[0, 0], 1e-30)
        shift = 14.0 - jnp.ceil(jnp.log2(bound))

        packed = pack(total, shift)
        terms, shifts = [lax.dynamic_slice_in_dim(total, chip * group, group, 1)], [shift]
        for k in range(1, chips):
            piece = lax.dynamic_slice_in_dim(packed, (chip ^ k) * group, group, 1)
            value, other = unpack(swap(piece, "node", nodes_axis, 2 * k))
            terms.append(value)
            shifts.append(other)
        forces = tree(terms)
        shift = jnp.min(jnp.stack(shifts)) - chip_bits

        for bit in range(field_axis.bit_length() - 1):
            value, other = unpack(swap(pack(forces, shift), "fld", field_axis, 1 << bit))
            forces = forces + value
            shift = jnp.minimum(shift, other) - 1.0

        wmod = lax.dynamic_slice_in_dim(omega_mode, core * width, width)[None, :]
        damp = lax.dynamic_slice_in_dim(damping, core * width, width)[None, :]
        wcol = jnp.repeat(omega_force, half // omega_force.shape[0])
        wcol = lax.dynamic_slice_in_dim(wcol, chip * group, group)[:, None]
        real_part = wmod * wmod - wcol * wcol
        imag_part = 2.0 * damp * wmod * wcol
        magnitude = real_part * real_part + imag_part * imag_part
        h_real = real_part / magnitude
        h_imag = -imag_part / magnitude
        a_real = h_real * forces[0] - h_imag * forces[1]
        a_imag = h_real * forces[1] + h_imag * forces[0]
        response = jnp.stack([a_real, a_imag]).astype(BF16)

        slots = [response] + [swap(response, "node", nodes_axis, 2 * k) for k in range(1, chips)]
        slots += [swap(slot, "node", nodes_axis, 1) for slot in slots]
        if group % 16:
            order = chip ^ jnp.arange(chips)
            slots = [
                jnp.moveaxis(jnp.stack(side)[order], 0, 1).reshape(2, half, width)
                for side in (slots[:chips], slots[chips:])
            ]

        sums = panel_sums(place, slots, *panel_modes(panel_of, modes))
        pieces = [sums] + [swap(sums, "fld", field_axis, k) for k in range(1, field_axis)]
        field = field_sums(place, pieces, *radiation(omega_force, dist_bin.T))
        field = field + swap(field, "node", nodes_axis, 1)
        return tree([field] + [swap(field, "node", nodes_axis, 2 * k) for k in range(1, chips)])

    return body


def solution(mesh):
    in_specs = (
        P(("node", "fld"), None),
        P(("node", "fld"), None),
        P(),
        P(),
        P(),
        P(("node", "fld")),
        P("node", "fld"),
    )
    out_specs = P("fld", None)
    body = shards(mesh.shape["node"], mesh.shape["fld"])
    return jax.shard_map(body, mesh=mesh, in_specs=in_specs, out_specs=out_specs, check_vma=False)
```

```python
import functools
import math

import jax
import jax.numpy as jnp
from jax import lax
from jax.experimental import pallas as pl
from jax.experimental.pallas import tpu as pltpu
from jax.sharding import PartitionSpec as P

PANEL_DEV = 256
BF16, F16, F32 = jnp.bfloat16, jnp.float16, jnp.float32
NT = (((1,), (1,)), ((), ()))
MIB = 1024 * 1024


def row_block(rows):
    return next(b for b in (256, 128, 64, 32, 16, rows) if rows % b == 0)


def start_rows(modes_ref, held_ref, sems, first):
    nodes, width = held_ref.shape
    rows = nodes // sems.shape[0]
    copies = []
    for k in range(sems.shape[0]):
        block = pl.ds(k * rows, rows)
        copies.append(
            pltpu.make_async_copy(
                modes_ref.at[block, pl.ds(first, width)], held_ref.at[block, :], sems.at[k]
            )
        )
        copies[-1].start()
    return rows, copies


def forces_sums(half_ref, left_ref, modes_ref, out_ref, top_ref, held_ref, sems, ready):
    width = held_ref.shape[1]
    rows, copies = start_rows(modes_ref, held_ref, sems, pl.multiple_of(half_ref[0] * width, 128))
    ready()
    for k, copy in enumerate(copies):
        copy.wait()
        block = slice(k * rows, (k + 1) * rows)
        part = jnp.dot(left_ref[:, block], held_ref[block, :], preferred_element_type=F32)
        for t in range(width // 128):
            tile = part[:, t * 128 : (t + 1) * 128]
            out_ref[t] = tile if k == 0 else out_ref[t] + tile
    top_ref[...] = jnp.full(top_ref.shape, jnp.max(jnp.abs(out_ref[...])), F32)


def first_kernel(half_ref, pressure_ref, modes_ref, out_ref, top_ref, left_ref, loads_ref, held_ref, sem, sems):
    load = pltpu.make_async_copy(pressure_ref, loads_ref, sem)
    load.start()

    def ready():
        load.wait()
        left_ref[...] = loads_ref[...].T

    forces_sums(half_ref, left_ref, modes_ref, out_ref, top_ref, held_ref, sems, ready)


def second_kernel(half_ref, left_ref, modes_ref, out_ref, top_ref, held_ref, sems):
    forces_sums(half_ref, left_ref, modes_ref, out_ref, top_ref, held_ref, sems, lambda: None)


def forces_half(half, pressure, modes, first):
    nodes, columns = pressure.shape if first else pressure.shape[::-1]
    width = modes.shape[1] // 2
    vmem, hbm = pl.BlockSpec(memory_space=pltpu.VMEM), pl.BlockSpec(memory_space=pltpu.HBM)
    outs = [
        jax.ShapeDtypeStruct((width // 128, columns, 128), F32),
        jax.ShapeDtypeStruct((8, 128), F32),
        jax.ShapeDtypeStruct((columns, nodes), BF16),
    ][: 3 if first else 2]
    scratch = [
        pltpu.VMEM((nodes, columns), BF16),
        pltpu.VMEM((nodes, width), BF16),
        pltpu.SemaphoreType.DMA,
        pltpu.SemaphoreType.DMA((nodes // row_block(nodes),)),
    ]
    return pl.pallas_call(
        first_kernel if first else second_kernel,
        in_specs=[pl.BlockSpec(memory_space=pltpu.SMEM), hbm if first else vmem, hbm],
        out_specs=[vmem] * len(outs),
        out_shape=outs,
        scratch_shapes=scratch if first else scratch[1::2],
        compiler_params=pltpu.CompilerParams(vmem_limit_bytes=51 * MIB),
        cost_estimate=pl.CostEstimate(
            flops=2 * nodes * columns * width, bytes_accessed=2 * nodes * width, transcendentals=0
        ),
        name="forces_half",
    )(half, pressure, modes)


def panel_modes_kernel(half, panel_ref, modes_ref, high_ref, low_ref, onehot_ref, held_ref, total_ref, sems):
    width = held_ref.shape[1]
    rows, copies = start_rows(modes_ref, held_ref, sems, half * width)
    panels = lax.broadcasted_iota(jnp.int32, onehot_ref.shape, 0)
    onehot_ref[...] = jnp.where(panels == panel_ref[...], 1.0, 0.0).astype(BF16)
    for k, copy in enumerate(copies):
        copy.wait()
        block = slice(k * rows, (k + 1) * rows)
        part = jnp.dot(onehot_ref[:, block], held_ref[block, :], preferred_element_type=F32)
        total_ref[...] = part if k == 0 else total_ref[...] + part
    total = total_ref[...]
    high = total.astype(BF16)
    high_ref[...] = high
    low_ref[...] = (total - high.astype(F32)).astype(BF16)


def panel_modes(half, panel_of, modes):
    nodes, count = modes.shape
    width = count // 2
    blocks = 4 if nodes % 64 == 0 else 1
    return pl.pallas_call(
        functools.partial(panel_modes_kernel, half),
        in_specs=[pl.BlockSpec(memory_space=pltpu.VMEM), pl.BlockSpec(memory_space=pltpu.HBM)],
        out_specs=[pl.BlockSpec(memory_space=pltpu.VMEM)] * 2,
        out_shape=[jax.ShapeDtypeStruct((PANEL_DEV, width), BF16)] * 2,
        scratch_shapes=[
            pltpu.VMEM((PANEL_DEV, nodes), BF16),
            pltpu.VMEM((nodes, width), BF16),
            pltpu.VMEM((PANEL_DEV, width), F32),
            pltpu.SemaphoreType.DMA((blocks,)),
        ],
        compiler_params=pltpu.CompilerParams(vmem_limit_bytes=51 * MIB),
        cost_estimate=pl.CostEstimate(
            flops=2 * nodes * PANEL_DEV * width, bytes_accessed=2 * nodes * width, transcendentals=0
        ),
        name="panel_modes",
    )(panel_of.reshape(1, nodes), modes)


def sin_cos(angle):
    turns = jnp.floor(angle * (2.0 / math.pi) + 0.5)
    rest = angle - turns * 1.5703125
    rest = rest - turns * 4.837512969970703125e-4
    rest = rest - turns * 7.549789948768648e-8
    square = rest * rest
    sine = rest + rest * square * (
        -1.6666654611e-1 + square * (8.3321608736e-3 - square * 1.9515295891e-4)
    )
    cosine = (1.0 - 0.5 * square) + square * square * (
        4.166664568298827e-2 + square * (-1.388731625493765e-3 + square * 2.443315711809948e-5)
    )
    quadrant = turns.astype(jnp.int32)
    swap = (quadrant & 1) == 1
    sin_sign = jnp.where((quadrant & 2) == 2, -1.0, 1.0)
    cos_sign = jnp.where(((quadrant + 1) & 2) == 2, -1.0, 1.0)
    return jnp.where(swap, cosine, sine) * sin_sign, jnp.where(swap, sine, cosine) * cos_sign


def radiation_kernel(first, omega_ref, bins_ref, high_ref, low_ref, dist_ref):
    pair = pl.program_id(0)

    @pl.when(pair == 0)
    def _():
        dist = 1.0 + 0.05 * bins_ref[...].astype(F32)
        dist_ref[...] = jnp.concatenate([dist, dist], axis=0).T

    dist = dist_ref[...]
    lane = lax.broadcasted_iota(jnp.int32, (1, dist.shape[1]), 1)
    freq = first + 2 * pair
    omega = jnp.where(lane < dist.shape[1] // 2, omega_ref[freq], omega_ref[freq + 1])
    sine, cosine = sin_cos(omega * dist)
    gain = (-0.01 / (2.0 * math.pi)) * omega * omega / dist
    for part, value in enumerate((gain * cosine, -gain * sine)):
        high = value.astype(BF16)
        high_ref[part] = high
        low_ref[part] = (value - high.astype(F32)).astype(BF16)


def radiation(first, count, omega_force, bins):
    field, panels = bins.shape
    return pl.pallas_call(
        functools.partial(radiation_kernel, first),
        grid=(count // 2,),
        in_specs=[
            pl.BlockSpec(memory_space=pltpu.SMEM),
            pl.BlockSpec((field, panels), lambda q: (0, 0)),
        ],
        out_specs=[pl.BlockSpec((2, panels, 2 * field), lambda q: (0, 0, q))] * 2,
        out_shape=[jax.ShapeDtypeStruct((2, panels, count * field), BF16)] * 2,
        scratch_shapes=[pltpu.VMEM((panels, 2 * field), F32)],
        compiler_params=pltpu.CompilerParams(vmem_limit_bytes=16 * MIB),
        cost_estimate=pl.CostEstimate(
            flops=40 * count * field * panels, bytes_accessed=4 * count * field * panels, transcendentals=0
        ),
        name="radiation",
    )(omega_force, bins)


def panel_sums_kernel(place_ref, *refs):
    *slots, high0, low0, high1, low1, out_ref, held_ref = refs
    core, chip = place_ref[0], place_ref[1]
    count = len(slots) // 2
    tiles, _, group, lanes = slots[0].shape
    half = held_ref.shape[1] // 2
    for side in range(2):
        for k in range(count):
            slot = slots[side * count + k]
            start = 0 if count == 1 else pl.multiple_of((chip ^ k) * group, group)
            for part in range(2):
                for t in range(tiles):
                    held_ref[core ^ side, pl.ds(part * half + start, group), t * lanes : (t + 1) * lanes] = slot[t, part]
    total = None
    for side, pair in enumerate(((high0, low0), (high1, low1))):
        for ref in pair:
            term = lax.dot_general(held_ref[side], ref[...], NT, preferred_element_type=F32)
            total = term if total is None else total + term
    out_ref[...] = total.astype(out_ref.dtype)


def panel_sums(place, slots, first, second):
    half = slots[0].shape[2] * (len(slots) // 2)
    width = slots[0].shape[0] * slots[0].shape[3]
    vmem = pl.BlockSpec(memory_space=pltpu.VMEM)
    return pl.pallas_call(
        panel_sums_kernel,
        in_specs=[pl.BlockSpec(memory_space=pltpu.SMEM)] + [vmem] * (len(slots) + 4),
        out_specs=vmem,
        out_shape=jax.ShapeDtypeStruct((2 * half, PANEL_DEV), BF16),
        scratch_shapes=[pltpu.VMEM((2, 2 * half, width), BF16)],
        compiler_params=pltpu.CompilerParams(vmem_limit_bytes=16 * MIB),
        name="panel_sums",
    )(place, *slots, *first, *second)


def field_kernel(freqs, place_ref, *refs):
    *pieces, high0, low0, high1, low1, out_ref = refs
    own = place_ref[2]
    columns = pieces[0].shape[0]
    half = columns // 2
    field = out_ref.shape[0]
    wide = 2 * field
    parts = [None] * 4
    for k, piece in enumerate(pieces):
        rows = pl.ds(pl.multiple_of((own ^ k) * PANEL_DEV, PANEL_DEV), PANEL_DEV)
        for part in range(2):
            for side, pair in enumerate(((high0, low0), (high1, low1))):
                for ref in pair:
                    term = jnp.dot(piece[...], ref[part, rows, :], preferred_element_type=F32)
                    at = 2 * part + side
                    parts[at] = term if parts[at] is None else parts[at] + term
    row = lax.broadcasted_iota(jnp.int32, (columns, wide), 0)
    freq_of = (row % half) // (half // freqs)
    sums = []
    for part in range(2):
        picked = None
        for pair in range(freqs // 2):
            side, at = divmod(pair, freqs // 4)
            block = parts[2 * part + side][:, at * wide : (at + 1) * wide]
            picked = block if picked is None else jnp.where(freq_of // 2 == pair, block, picked)
        sums.append(jnp.where(freq_of % 2 == 1, pltpu.roll(picked, field, 1), picked))
    real = sums[0][:half] - sums[1][half:]
    imag = sums[0][half:] + sums[1][:half]
    out_ref[...] = jnp.concatenate([real, imag], axis=0).T[:field]


def field_sums(freqs, field, place, pieces, first, second):
    columns = pieces[0].shape[0]
    vmem = pl.BlockSpec(memory_space=pltpu.VMEM)
    return pl.pallas_call(
        functools.partial(field_kernel, freqs),
        in_specs=[pl.BlockSpec(memory_space=pltpu.SMEM)] + [vmem] * (len(pieces) + 4),
        out_specs=vmem,
        out_shape=jax.ShapeDtypeStruct((field, columns), F32),
        compiler_params=pltpu.CompilerParams(vmem_limit_bytes=24 * MIB),
        name="field_sums",
    )(place, *pieces, *first, *second)


def tree(terms):
    while len(terms) > 1:
        terms = [a + b for a, b in zip(terms[::2], terms[1::2], strict=True)]
    return terms[0]


def swap(x, axis, size, k):
    return lax.ppermute(x, axis, [(i, i ^ k) for i in range(size)])


def pack(x, shift):
    scaled = (x * jnp.exp2(shift)).astype(F16)
    note = jnp.broadcast_to(shift, (1, *x.shape[1:])).astype(F16)
    return jnp.concatenate([scaled, note], axis=0)


def unpack(y):
    shift = y[-1:].astype(F32)
    return y[:-1].astype(F32) * jnp.exp2(-shift), shift


def beside(x, work):
    return lax.optimization_barrier((x, work))


def shards(nodes_axis, field_axis):
    chips = nodes_axis // 2
    chip_bits = chips.bit_length() - 1

    def body(pressure, modes, omega_mode, damping, omega_force, panel_of, dist_bin):
        columns = pressure.shape[1]
        half = columns // 2
        width = modes.shape[1] // 2
        tiles = width // 128
        group = half // chips
        node = lax.axis_index("node")
        core, chip, fld = node % 2, node // 2, lax.axis_index("fld")
        place = jnp.stack([core, chip, fld]).astype(jnp.int32)

        away, away_top, left = forces_half((1 - core).reshape(1), pressure, modes, True)
        came, came_top = (swap(x, "node", nodes_axis, 1) for x in (away, away_top))
        home, home_top = forces_half(core.reshape(1), left, modes, False)
        total = (home + came).reshape(tiles, 2, half, 128)
        bound = jnp.maximum(home_top[:1] + came_top[:1], 1e-30)
        shift = jnp.broadcast_to(14.0 - jnp.ceil(jnp.log2(bound)), (1, 2, group, 128))

        packed, panel_known = beside(pack(total, shift[:, :, :1]), panel_of)
        came = [
            swap(lax.dynamic_slice_in_dim(packed, (chip ^ k) * group, group, 2), "node", nodes_axis, 2 * k)
            for k in range(1, chips)
        ]
        came, first = beside(came, panel_modes(0, panel_known, modes))
        terms, shifts = [lax.dynamic_slice_in_dim(total, chip * group, group, 2)], [shift]
        for piece in came:
            value, other = unpack(piece)
            terms.append(value)
            shifts.append(other)
        forces = tree(terms)
        shift = functools.reduce(jnp.minimum, shifts) - chip_bits

        freqs = omega_force.shape[0]
        bins, kernels = dist_bin.T, []
        steps = field_axis.bit_length() - 1
        for bit in range(steps):
            packed, bins = beside(pack(forces, shift), bins)
            came = swap(packed, "fld", field_axis, 1 << bit)
            if bit < 2:
                came, kernel = beside(came, radiation(bit * freqs // 2, freqs // 2, omega_force, bins))
                kernels.append(kernel)
            value, other = unpack(came)
            forces = forces + value
            shift = jnp.minimum(shift, other) - 1.0
        for rest in range(len(kernels), 2):
            kernels.append(radiation(rest * freqs // 2, freqs // 2, omega_force, bins))

        wmod = lax.dynamic_slice_in_dim(omega_mode, core * width, width).reshape(tiles, 1, 128)
        damp = lax.dynamic_slice_in_dim(damping, core * width, width).reshape(tiles, 1, 128)
        wcol = jnp.repeat(omega_force, half // omega_force.shape[0])
        wcol = lax.dynamic_slice_in_dim(wcol, chip * group, group)[None, :, None]
        real_part = wmod * wmod - wcol * wcol
        imag_part = 2.0 * damp * wmod * wcol
        magnitude = real_part * real_part + imag_part * imag_part
        h_real = real_part / magnitude
        h_imag = -imag_part / magnitude
        a_real = h_real * forces[:, 0] - h_imag * forces[:, 1]
        a_imag = h_real * forces[:, 1] + h_imag * forces[:, 0]
        response = jnp.stack([a_real, a_imag], axis=1).astype(BF16)

        response, panel_known = beside(response, panel_known)
        came = [swap(response, "node", nodes_axis, 2 * k) for k in range(1, chips)]
        came, second = beside(came, panel_modes(1, panel_known, modes))
        slots = [response, *came]
        slots += [swap(slot, "node", nodes_axis, 1) for slot in slots]
        if group % 16:
            order = chip ^ jnp.arange(chips)
            slots = [
                jnp.moveaxis(jnp.stack(side)[order], 0, 2).reshape(tiles, 2, half, 128)
                for side in (slots[:chips], slots[chips:])
            ]

        sums = panel_sums(place, slots, first, second)
        pieces = [sums] + [swap(sums, "fld", field_axis, k) for k in range(1, field_axis)]
        field = field_sums(freqs, dist_bin.shape[1], place, pieces, *kernels)
        field = field + swap(field, "node", nodes_axis, 1)
        return tree([field] + [swap(field, "node", nodes_axis, 2 * k) for k in range(1, chips)])

    return body


def solution(mesh):
    in_specs = (
        P(("node", "fld"), None),
        P(("node", "fld"), None),
        P(),
        P(),
        P(),
        P(("node", "fld")),
        P("node", "fld"),
    )
    out_specs = P("fld", None)
    body = shards(mesh.shape["node"], mesh.shape["fld"])
    return jax.shard_map(body, mesh=mesh, in_specs=in_specs, out_specs=out_specs, check_vma=False)
```

```python
import functools
import math

import jax
import jax.numpy as jnp
from jax import lax
from jax.experimental import pallas as pl
from jax.experimental.pallas import tpu as pltpu
from jax.sharding import PartitionSpec as P

PANEL_DEV = 256
BF16, F16, F32 = jnp.bfloat16, jnp.float16, jnp.float32
NT = (((1,), (1,)), ((), ()))
MIB = 1024 * 1024


def row_block(rows):
    return next(b for b in (256, 128, 64, 32, 16, rows) if rows % b == 0)


def start_rows(modes_ref, held_ref, sems, first):
    nodes, width = held_ref.shape
    rows = nodes // sems.shape[0]
    copies = []
    for k in range(sems.shape[0]):
        block = pl.ds(k * rows, rows)
        copies.append(
            pltpu.make_async_copy(
                modes_ref.at[block, pl.ds(first, width)], held_ref.at[block, :], sems.at[k]
            )
        )
        copies[-1].start()
    return rows, copies


def forces_sums(half_ref, left_ref, modes_ref, out_ref, top_ref, held_ref, sems, ready):
    width = held_ref.shape[1]
    rows, copies = start_rows(modes_ref, held_ref, sems, pl.multiple_of(half_ref[0] * width, 128))
    ready()
    for k, copy in enumerate(copies):
        copy.wait()
        block = slice(k * rows, (k + 1) * rows)
        part = jnp.dot(left_ref[:, block], held_ref[block, :], preferred_element_type=F32)
        for t in range(width // 128):
            tile = part[:, t * 128 : (t + 1) * 128]
            out_ref[t] = tile if k == 0 else out_ref[t] + tile
    top_ref[...] = jnp.full(top_ref.shape, jnp.max(jnp.abs(out_ref[...])), F32)


def first_kernel(half_ref, pressure_ref, modes_ref, out_ref, top_ref, left_ref, loads_ref, held_ref, sem, sems):
    load = pltpu.make_async_copy(pressure_ref, loads_ref, sem)
    load.start()

    def ready():
        load.wait()
        rows = loads_ref.shape[1]
        for k in range(loads_ref.shape[0]):
            left_ref[:, k * rows : (k + 1) * rows] = loads_ref[k].T

    forces_sums(half_ref, left_ref, modes_ref, out_ref, top_ref, held_ref, sems, ready)


def second_kernel(half_ref, left_ref, modes_ref, out_ref, top_ref, held_ref, sems):
    forces_sums(half_ref, left_ref, modes_ref, out_ref, top_ref, held_ref, sems, lambda: None)


def forces_half(half, pressure, modes, first):
    columns, nodes = (pressure.shape[2], modes.shape[0]) if first else pressure.shape
    width = modes.shape[1] // 2
    vmem, hbm = pl.BlockSpec(memory_space=pltpu.VMEM), pl.BlockSpec(memory_space=pltpu.HBM)
    outs = [
        jax.ShapeDtypeStruct((width // 128, columns, 128), F32),
        jax.ShapeDtypeStruct((8, 128), F32),
        jax.ShapeDtypeStruct((columns, nodes), BF16),
    ][: 3 if first else 2]
    scratch = [
        pltpu.VMEM(pressure.shape, BF16),
        pltpu.VMEM((nodes, width), BF16),
        pltpu.SemaphoreType.DMA,
        pltpu.SemaphoreType.DMA((nodes // row_block(nodes),)),
    ]
    return pl.pallas_call(
        first_kernel if first else second_kernel,
        in_specs=[pl.BlockSpec(memory_space=pltpu.SMEM), hbm if first else vmem, hbm],
        out_specs=[vmem] * len(outs),
        out_shape=outs,
        scratch_shapes=scratch if first else scratch[1::2],
        compiler_params=pltpu.CompilerParams(vmem_limit_bytes=51 * MIB),
        cost_estimate=pl.CostEstimate(
            flops=2 * nodes * columns * width, bytes_accessed=2 * nodes * width, transcendentals=0
        ),
        name="forces_half",
    )(half, pressure, modes)


def panel_modes_kernel(half_ref, panel_ref, modes_ref, high_ref, low_ref, onehot_ref, held_ref, total_ref, sems):
    width = held_ref.shape[1]
    rows, copies = start_rows(modes_ref, held_ref, sems, pl.multiple_of(half_ref[0] * width, 128))
    panels = lax.broadcasted_iota(jnp.int32, onehot_ref.shape, 0)
    onehot_ref[...] = jnp.where(panels == panel_ref[...], 1.0, 0.0).astype(BF16)
    for k, copy in enumerate(copies):
        copy.wait()
        block = slice(k * rows, (k + 1) * rows)
        part = jnp.dot(onehot_ref[:, block], held_ref[block, :], preferred_element_type=F32)
        total_ref[...] = part if k == 0 else total_ref[...] + part
    total = total_ref[...]
    high = total.astype(BF16)
    high_ref[...] = high
    low_ref[...] = (total - high.astype(F32)).astype(BF16)


def panel_modes(half, panel_of, modes):
    nodes, count = modes.shape
    width = count // 2
    blocks = 4 if nodes % 64 == 0 else 1
    return pl.pallas_call(
        panel_modes_kernel,
        in_specs=[
            pl.BlockSpec(memory_space=pltpu.SMEM),
            pl.BlockSpec(memory_space=pltpu.VMEM),
            pl.BlockSpec(memory_space=pltpu.HBM),
        ],
        out_specs=[pl.BlockSpec(memory_space=pltpu.VMEM)] * 2,
        out_shape=[jax.ShapeDtypeStruct((PANEL_DEV, width), BF16)] * 2,
        scratch_shapes=[
            pltpu.VMEM((PANEL_DEV, nodes), BF16),
            pltpu.VMEM((nodes, width), BF16),
            pltpu.VMEM((PANEL_DEV, width), F32),
            pltpu.SemaphoreType.DMA((blocks,)),
        ],
        compiler_params=pltpu.CompilerParams(vmem_limit_bytes=51 * MIB),
        cost_estimate=pl.CostEstimate(
            flops=2 * nodes * PANEL_DEV * width, bytes_accessed=2 * nodes * width, transcendentals=0
        ),
        name="panel_modes",
    )(half, panel_of.reshape(1, nodes), modes)


def sin_cos(angle):
    turns = jnp.floor(angle * (2.0 / math.pi) + 0.5)
    rest = angle - turns * 1.5703125
    rest = rest - turns * 4.837512969970703125e-4
    rest = rest - turns * 7.549789948768648e-8
    square = rest * rest
    sine = rest + rest * square * (
        -1.6666654611e-1 + square * (8.3321608736e-3 - square * 1.9515295891e-4)
    )
    cosine = (1.0 - 0.5 * square) + square * square * (
        4.166664568298827e-2 + square * (-1.388731625493765e-3 + square * 2.443315711809948e-5)
    )
    quadrant = turns.astype(jnp.int32)
    swap = (quadrant & 1) == 1
    sin_sign = jnp.where((quadrant & 2) == 2, -1.0, 1.0)
    cos_sign = jnp.where(((quadrant + 1) & 2) == 2, -1.0, 1.0)
    return jnp.where(swap, cosine, sine) * sin_sign, jnp.where(swap, sine, cosine) * cos_sign


def radiation_kernel(first, omega_ref, bins_ref, high_ref, low_ref, dist_ref):
    pair = pl.program_id(0)

    @pl.when(pair == 0)
    def _():
        dist = 1.0 + 0.05 * bins_ref[...].astype(F32)
        dist_ref[...] = jnp.concatenate([dist, dist], axis=0).T

    dist = dist_ref[...]
    lane = lax.broadcasted_iota(jnp.int32, (1, dist.shape[1]), 1)
    freq = first + 2 * pair
    omega = jnp.where(lane < dist.shape[1] // 2, omega_ref[freq], omega_ref[freq + 1])
    sine, cosine = sin_cos(omega * dist)
    gain = (-0.01 / (2.0 * math.pi)) * omega * omega / dist
    for part, value in enumerate((gain * cosine, -gain * sine)):
        high = value.astype(BF16)
        high_ref[part] = high
        low_ref[part] = (value - high.astype(F32)).astype(BF16)


def radiation(first, count, omega_force, bins):
    field, panels = bins.shape
    return pl.pallas_call(
        functools.partial(radiation_kernel, first),
        grid=(count // 2,),
        in_specs=[
            pl.BlockSpec(memory_space=pltpu.SMEM),
            pl.BlockSpec((field, panels), lambda q: (0, 0)),
        ],
        out_specs=[pl.BlockSpec((2, panels, 2 * field), lambda q: (0, 0, q))] * 2,
        out_shape=[jax.ShapeDtypeStruct((2, panels, count * field), BF16)] * 2,
        scratch_shapes=[pltpu.VMEM((panels, 2 * field), F32)],
        compiler_params=pltpu.CompilerParams(vmem_limit_bytes=16 * MIB),
        cost_estimate=pl.CostEstimate(
            flops=40 * count * field * panels, bytes_accessed=4 * count * field * panels, transcendentals=0
        ),
        name="radiation",
    )(omega_force, bins)


def panel_sums_kernel(count, place_ref, *refs):
    slots, (high_ref, low_ref), before, (out_ref, held_ref) = refs[:count], refs[count : count + 2], refs[count + 2 : -2], refs[-2:]
    chip = place_ref[1]
    tiles, _, group, lanes = slots[0].shape
    half = held_ref.shape[0] // 2
    for k, slot in enumerate(slots):
        start = 0 if count == 1 else pl.multiple_of((chip ^ (count - 1 - k)) * group, group)
        for part in range(2):
            for t in range(tiles):
                held_ref[pl.ds(part * half + start, group), t * lanes : (t + 1) * lanes] = slot[t, part]
    total = before[0][...] if before else None
    for ref in (high_ref, low_ref):
        term = lax.dot_general(held_ref[...], ref[...], NT, preferred_element_type=F32)
        total = term if total is None else total + term
    out_ref[...] = total.astype(out_ref.dtype)


def panel_sums(place, slots, pair, *before):
    half = slots[0].shape[2] * len(slots)
    width = slots[0].shape[0] * slots[0].shape[3]
    vmem = pl.BlockSpec(memory_space=pltpu.VMEM)
    return pl.pallas_call(
        functools.partial(panel_sums_kernel, len(slots)),
        in_specs=[pl.BlockSpec(memory_space=pltpu.SMEM)] + [vmem] * (len(slots) + 2 + len(before)),
        out_specs=vmem,
        out_shape=jax.ShapeDtypeStruct((2 * half, PANEL_DEV), BF16 if before else F32),
        scratch_shapes=[pltpu.VMEM((2 * half, width), BF16)],
        compiler_params=pltpu.CompilerParams(vmem_limit_bytes=16 * MIB),
        cost_estimate=pl.CostEstimate(
            flops=8 * half * width * PANEL_DEV, bytes_accessed=8 * width * PANEL_DEV, transcendentals=0
        ),
        name="panel_sums",
    )(place, *slots, *pair, *before)


def field_kernel(freqs, order, place_ref, *refs):
    pieces, kernels, out_ref = refs[: len(order)], refs[len(order) : -1], refs[-1]
    own = place_ref[2]
    columns = pieces[0].shape[0]
    half = columns // 2
    field = out_ref.shape[0]
    wide = 2 * field
    products = [[None] * (len(kernels) // 2) for _ in range(2)]
    for k, piece in zip(order, pieces, strict=True):
        rows = pl.ds(pl.multiple_of((own ^ k) * PANEL_DEV, PANEL_DEV), PANEL_DEV)
        for part in range(2):
            for at, ref in enumerate(kernels):
                term = jnp.dot(piece[...], ref[part, rows, :], preferred_element_type=F32)
                before = products[part][at // 2]
                products[part][at // 2] = term if before is None else before + term
    row = lax.broadcasted_iota(jnp.int32, (columns, wide), 0)
    freq_of = (row % half) // (half // freqs)
    sums = []
    for part in range(2):
        blocks = [p[:, i : i + wide] for p in products[part] for i in range(0, p.shape[1], wide)]
        picked = blocks[0]
        for pair in range(1, freqs // 2):
            picked = jnp.where(freq_of // 2 == pair, blocks[pair], picked)
        sums.append(jnp.where(freq_of % 2 == 1, pltpu.roll(picked, field, 1), picked))
    real = sums[0][:half] - sums[1][half:]
    imag = sums[0][half:] + sums[1][:half]
    out_ref[...] = jnp.concatenate([real, imag], axis=0).T[:field]


def field_sums(freqs, field, place, pieces, kernels):
    columns = pieces[0].shape[0]
    vmem = pl.BlockSpec(memory_space=pltpu.VMEM)
    return pl.pallas_call(
        functools.partial(field_kernel, freqs, tuple(pieces)),
        in_specs=[pl.BlockSpec(memory_space=pltpu.SMEM)] + [vmem] * (len(pieces) + len(kernels)),
        out_specs=vmem,
        out_shape=jax.ShapeDtypeStruct((field, columns), F32),
        compiler_params=pltpu.CompilerParams(vmem_limit_bytes=24 * MIB),
        name="field_sums",
    )(place, *pieces.values(), *kernels)


def tree(terms):
    while len(terms) > 1:
        terms = [a + b for a, b in zip(terms[::2], terms[1::2], strict=True)]
    return terms[0]


def swap(x, axis, size, k):
    return lax.ppermute(x, axis, [(i, i ^ k) for i in range(size)])


def far_first(size):
    return range(size - 1, 0, -1)


def pack(x, shift):
    scaled = (x * jnp.exp2(shift)).astype(F16).reshape(-1, x.shape[-1])
    note = jnp.broadcast_to(shift.reshape(1, -1), (8, x.shape[-1])).astype(F16)
    return jnp.concatenate([scaled, note], axis=0)


def unpack(y, shape):
    shift = y[-8:-7].astype(F32).reshape(1, 1, 1, -1)
    return y[:-8].reshape(shape).astype(F32) * jnp.exp2(-shift), shift


def beside(x, work):
    return lax.optimization_barrier((x, work))


def shards(nodes_axis, field_axis):
    chips = nodes_axis // 2
    chip_bits = chips.bit_length() - 1

    def body(pressure, modes, omega_mode, damping, omega_force, panel_of, dist_bin):
        columns = pressure.shape[1]
        half = columns // 2
        width = modes.shape[1] // 2
        tiles = width // 128
        group = half // chips
        node = lax.axis_index("node")
        core, chip, fld = node % 2, node // 2, lax.axis_index("fld")
        place = jnp.stack([core, chip, fld]).astype(jnp.int32)

        away, away_top, left = forces_half(
            (1 - core).reshape(1), pressure.reshape(-1, row_block(pressure.shape[0]), columns), modes, True
        )
        came, came_top = (swap(x, "node", nodes_axis, 1) for x in (away, away_top))
        home, home_top = forces_half(core.reshape(1), left, modes, False)
        total = (home + came).reshape(tiles, 2, half, 128)
        bound = jnp.maximum(home_top[:1] + came_top[:1], 1e-30)
        shift = (14.0 - jnp.ceil(jnp.log2(bound))).reshape(1, 1, 1, 128)

        share = (tiles, 2, group, 128)
        sent = [
            pack(lax.dynamic_slice_in_dim(total, (chip ^ k) * group, group, 2), shift) for k in far_first(chips)
        ]
        sent, panel_known = beside(sent, panel_of)
        came = [swap(piece, "node", nodes_axis, 2 * k) for k, piece in zip(far_first(chips), sent, strict=True)]
        came, first = beside(came, panel_modes(core.reshape(1), panel_known, modes))
        terms, shifts = [], [shift]
        for piece in came:
            value, other = unpack(piece, share)
            terms.append(value)
            shifts.append(other)
        forces = tree(terms + [lax.dynamic_slice_in_dim(total, chip * group, group, 2)])
        shift = functools.reduce(jnp.minimum, shifts) - chip_bits

        freqs = omega_force.shape[0]
        bins, kernels = dist_bin.T, []
        for bit in range(field_axis.bit_length() - 1):
            packed, bins = beside(pack(forces, shift), bins)
            came = swap(packed, "fld", field_axis, 1 << bit)
            if bit < 2:
                came, kernel = beside(came, radiation(2 * bit, 2, omega_force, bins))
                kernels.extend(kernel)
            value, other = unpack(came, share)
            forces = forces + value
            shift = jnp.minimum(shift, other) - 1.0

        wmod = lax.dynamic_slice_in_dim(omega_mode, core * width, width).reshape(tiles, 1, 128)
        damp = lax.dynamic_slice_in_dim(damping, core * width, width).reshape(tiles, 1, 128)
        wcol = jnp.repeat(omega_force, half // omega_force.shape[0])
        wcol = lax.dynamic_slice_in_dim(wcol, chip * group, group)[None, :, None]
        real_part = wmod * wmod - wcol * wcol
        imag_part = 2.0 * damp * wmod * wcol
        magnitude = real_part * real_part + imag_part * imag_part
        h_real = real_part / magnitude
        h_imag = -imag_part / magnitude
        a_real = h_real * forces[:, 0] - h_imag * forces[:, 1]
        a_imag = h_real * forces[:, 1] + h_imag * forces[:, 0]
        response = jnp.stack([a_real, a_imag], axis=1).astype(BF16)

        response, panel_known = beside(response, panel_known)
        came = [swap(response, "node", nodes_axis, 2 * k) for k in far_first(chips)]
        came, second = beside(came, panel_modes((1 - core).reshape(1), panel_known, modes))
        sides = [[*came, response]]
        sides.append([swap(slot, "node", nodes_axis, 1) for slot in sides[0]])
        if group % 16:
            order = chips - 1 - (chip ^ jnp.arange(chips))
            sides = [
                [jnp.moveaxis(jnp.stack(side)[order], 0, 2).reshape(tiles, 2, half, 128)] for side in sides
            ]
        sums = panel_sums(place, sides[0], first)
        sums = panel_sums(place, sides[1], second, sums)
        sums, bins = beside(sums, bins)
        pieces = {k: swap(sums, "fld", field_axis, k) for k in (2, 3, 1)} | {0: sums}
        done = sum(x.shape[2] // dist_bin.shape[1] for x in kernels[::2])
        kernels.extend(radiation(done, freqs - done, omega_force, bins))
        field = field_sums(freqs, dist_bin.shape[1], place, pieces, kernels)
        field = field + swap(field, "node", nodes_axis, 1)
        return tree([swap(field, "node", nodes_axis, 2 * k) for k in far_first(chips)] + [field])

    return body


def solution(mesh):
    in_specs = (
        P(("node", "fld"), None),
        P(("node", "fld"), None),
        P(),
        P(),
        P(),
        P(("node", "fld")),
        P("node", "fld"),
    )
    out_specs = P("fld", None)
    body = shards(mesh.shape["node"], mesh.shape["fld"])
    return jax.shard_map(body, mesh=mesh, in_specs=in_specs, out_specs=out_specs, check_vma=False)
```

```python
import functools
import math

import jax
import jax.numpy as jnp
from jax import lax
from jax.experimental import pallas as pl
from jax.experimental.pallas import tpu as pltpu
from jax.sharding import PartitionSpec as P

PANEL_DEV = 256
BF16, F16, F32 = jnp.bfloat16, jnp.float16, jnp.float32
NT = (((1,), (1,)), ((), ()))
MIB = 1024 * 1024


def row_block(rows):
    return next(b for b in (256, 128, 64, 32, 16, rows) if rows % b == 0)


def start_rows(modes_ref, held_ref, sems, first):
    nodes, width = held_ref.shape
    rows = nodes // sems.shape[0]
    copies = []
    for k in range(sems.shape[0]):
        block = pl.ds(k * rows, rows)
        copies.append(
            pltpu.make_async_copy(
                modes_ref.at[block, pl.ds(first, width)], held_ref.at[block, :], sems.at[k]
            )
        )
        copies[-1].start()
    return rows, copies


def forces_sums(left_ref, block_of, copies, rows, out_ref, top_ref):
    for k in range(left_ref.shape[1] // rows):
        if copies:
            copies[k].wait()
        block = slice(k * rows, (k + 1) * rows)
        part = jnp.dot(left_ref[:, block], block_of(block), preferred_element_type=F32)
        for t in range(out_ref.shape[0]):
            tile = part[:, t * 128 : (t + 1) * 128]
            out_ref[t] = tile if k == 0 else out_ref[t] + tile
    top_ref[...] = jnp.full(top_ref.shape, jnp.max(jnp.abs(out_ref[...])), F32)


def first_kernel(half_ref, pressure_ref, modes_ref, out_ref, top_ref, left_ref, loads_ref, held_ref, sem, sems):
    load = pltpu.make_async_copy(pressure_ref, loads_ref, sem)
    load.start()
    width = held_ref.shape[1]
    rows, copies = start_rows(modes_ref, held_ref, sems, pl.multiple_of(half_ref[0] * width, 128))
    load.wait()
    for k in range(loads_ref.shape[0]):
        part = loads_ref.shape[1]
        left_ref[:, k * part : (k + 1) * part] = loads_ref[k].T
    forces_sums(left_ref, lambda block: held_ref[block, :], copies, rows, out_ref, top_ref)


def second_kernel(half_ref, left_ref, modes_ref, out_ref, top_ref):
    width = modes_ref.shape[1] // 2
    columns = pl.ds(pl.multiple_of(half_ref[0] * width, 128), width)
    forces_sums(left_ref, lambda block: modes_ref[block, columns], None, row_block(left_ref.shape[1]), out_ref, top_ref)


def forces_half(half, pressure, modes, first):
    columns, nodes = (pressure.shape[2], modes.shape[0]) if first else pressure.shape
    width = modes.shape[1] // 2
    vmem, hbm = pl.BlockSpec(memory_space=pltpu.VMEM), pl.BlockSpec(memory_space=pltpu.HBM)
    outs = [
        jax.ShapeDtypeStruct((width // 128, columns, 128), F32),
        jax.ShapeDtypeStruct((8, 128), F32),
        jax.ShapeDtypeStruct((columns, nodes), BF16),
    ][: 3 if first else 2]
    scratch = [
        pltpu.VMEM(pressure.shape, BF16),
        pltpu.VMEM((nodes, width), BF16),
        pltpu.SemaphoreType.DMA,
        pltpu.SemaphoreType.DMA((nodes // row_block(nodes),)),
    ]
    if first:
        pressure, modes = (pltpu.with_memory_space_constraint(x, pltpu.HBM) for x in (pressure, modes))
    return pl.pallas_call(
        first_kernel if first else second_kernel,
        in_specs=[pl.BlockSpec(memory_space=pltpu.SMEM)] + ([hbm, hbm] if first else [vmem, vmem]),
        out_specs=[vmem] * len(outs),
        out_shape=outs,
        scratch_shapes=scratch if first else [],
        compiler_params=pltpu.CompilerParams(vmem_limit_bytes=16 * MIB),
        cost_estimate=pl.CostEstimate(
            flops=2 * nodes * columns * width, bytes_accessed=2 * nodes * width, transcendentals=0
        ),
        name="forces_half",
    )(half, pressure, modes)


def panel_modes_kernel(half_ref, panel_ref, modes_ref, high_ref, low_ref, onehot_ref, held_ref, total_ref, sems):
    width = held_ref.shape[1]
    rows, copies = start_rows(modes_ref, held_ref, sems, pl.multiple_of(half_ref[0] * width, 128))
    panels = lax.broadcasted_iota(jnp.int32, onehot_ref.shape, 0)
    onehot_ref[...] = jnp.where(panels == panel_ref[...], 1.0, 0.0).astype(BF16)
    for k, copy in enumerate(copies):
        copy.wait()
        block = slice(k * rows, (k + 1) * rows)
        part = jnp.dot(onehot_ref[:, block], held_ref[block, :], preferred_element_type=F32)
        total_ref[...] = part if k == 0 else total_ref[...] + part
    total = total_ref[...]
    high = total.astype(BF16)
    high_ref[...] = high
    low_ref[...] = (total - high.astype(F32)).astype(BF16)


def panel_modes(half, panel_of, modes):
    nodes, count = modes.shape
    width = count // 2
    blocks = 4 if nodes % 64 == 0 else 1
    return pl.pallas_call(
        panel_modes_kernel,
        in_specs=[
            pl.BlockSpec(memory_space=pltpu.SMEM),
            pl.BlockSpec(memory_space=pltpu.VMEM),
            pl.BlockSpec(memory_space=pltpu.HBM),
        ],
        out_specs=[pl.BlockSpec(memory_space=pltpu.VMEM)] * 2,
        out_shape=[jax.ShapeDtypeStruct((PANEL_DEV, width), BF16)] * 2,
        scratch_shapes=[
            pltpu.VMEM((PANEL_DEV, nodes), BF16),
            pltpu.VMEM((nodes, width), BF16),
            pltpu.VMEM((PANEL_DEV, width), F32),
            pltpu.SemaphoreType.DMA((blocks,)),
        ],
        compiler_params=pltpu.CompilerParams(vmem_limit_bytes=16 * MIB),
        cost_estimate=pl.CostEstimate(
            flops=2 * nodes * PANEL_DEV * width, bytes_accessed=2 * nodes * width, transcendentals=0
        ),
        name="panel_modes",
    )(half, panel_of.reshape(1, nodes), pltpu.with_memory_space_constraint(modes, pltpu.HBM))


def sin_cos(angle):
    turns = jnp.floor(angle * (2.0 / math.pi) + 0.5)
    rest = angle - turns * 1.5703125
    rest = rest - turns * 4.837512969970703125e-4
    rest = rest - turns * 7.549789948768648e-8
    square = rest * rest
    sine = rest + rest * square * (
        -1.6666654611e-1 + square * (8.3321608736e-3 - square * 1.9515295891e-4)
    )
    cosine = (1.0 - 0.5 * square) + square * square * (
        4.166664568298827e-2 + square * (-1.388731625493765e-3 + square * 2.443315711809948e-5)
    )
    quadrant = turns.astype(jnp.int32)
    swap = (quadrant & 1) == 1
    sin_sign = jnp.where((quadrant & 2) == 2, -1.0, 1.0)
    cos_sign = jnp.where(((quadrant + 1) & 2) == 2, -1.0, 1.0)
    return jnp.where(swap, cosine, sine) * sin_sign, jnp.where(swap, sine, cosine) * cos_sign


def radiation_kernel(first, omega_ref, bins_ref, high_ref, low_ref, dist_ref):
    pair = pl.program_id(0)

    @pl.when(pair == 0)
    def _():
        dist = 1.0 + 0.05 * bins_ref[...].astype(F32)
        dist_ref[...] = jnp.concatenate([dist, dist], axis=0).T

    dist = dist_ref[...]
    lane = lax.broadcasted_iota(jnp.int32, (1, dist.shape[1]), 1)
    freq = first + 2 * pair
    omega = jnp.where(lane < dist.shape[1] // 2, omega_ref[freq], omega_ref[freq + 1])
    sine, cosine = sin_cos(omega * dist)
    gain = (-0.01 / (2.0 * math.pi)) * omega * omega / dist
    for part, value in enumerate((gain * cosine, -gain * sine)):
        high = value.astype(BF16)
        high_ref[part] = high
        low_ref[part] = (value - high.astype(F32)).astype(BF16)


def radiation(first, count, omega_force, bins):
    field, panels = bins.shape
    return pl.pallas_call(
        functools.partial(radiation_kernel, first),
        grid=(count // 2,),
        in_specs=[
            pl.BlockSpec(memory_space=pltpu.SMEM),
            pl.BlockSpec((field, panels), lambda q: (0, 0)),
        ],
        out_specs=[pl.BlockSpec((2, panels, 2 * field), lambda q: (0, 0, q))] * 2,
        out_shape=[jax.ShapeDtypeStruct((2, panels, count * field), BF16)] * 2,
        scratch_shapes=[pltpu.VMEM((panels, 2 * field), F32)],
        compiler_params=pltpu.CompilerParams(vmem_limit_bytes=16 * MIB),
        cost_estimate=pl.CostEstimate(
            flops=40 * count * field * panels, bytes_accessed=4 * count * field * panels, transcendentals=0
        ),
        name="radiation",
    )(omega_force, bins)


def panel_sums_kernel(count, place_ref, *refs):
    slots, (high_ref, low_ref), before, (out_ref, held_ref) = refs[:count], refs[count : count + 2], refs[count + 2 : -2], refs[-2:]
    chip = place_ref[1]
    tiles, _, group, lanes = slots[0].shape
    half = held_ref.shape[0] // 2
    for k, slot in enumerate(slots):
        start = 0 if count == 1 else pl.multiple_of((chip ^ (count - 1 - k)) * group, group)
        for part in range(2):
            for t in range(tiles):
                held_ref[pl.ds(part * half + start, group), t * lanes : (t + 1) * lanes] = slot[t, part]
    total = before[0][...] if before else None
    for ref in (high_ref, low_ref):
        term = lax.dot_general(held_ref[...], ref[...], NT, preferred_element_type=F32)
        total = term if total is None else total + term
    out_ref[...] = total.astype(out_ref.dtype)


def panel_sums(place, slots, pair, *before):
    half = slots[0].shape[2] * len(slots)
    width = slots[0].shape[0] * slots[0].shape[3]
    vmem = pl.BlockSpec(memory_space=pltpu.VMEM)
    return pl.pallas_call(
        functools.partial(panel_sums_kernel, len(slots)),
        in_specs=[pl.BlockSpec(memory_space=pltpu.SMEM)] + [vmem] * (len(slots) + 2 + len(before)),
        out_specs=vmem,
        out_shape=jax.ShapeDtypeStruct((2 * half, PANEL_DEV), BF16 if before else F32),
        scratch_shapes=[pltpu.VMEM((2 * half, width), BF16)],
        compiler_params=pltpu.CompilerParams(vmem_limit_bytes=16 * MIB),
        cost_estimate=pl.CostEstimate(
            flops=8 * half * width * PANEL_DEV, bytes_accessed=8 * width * PANEL_DEV, transcendentals=0
        ),
        name="panel_sums",
    )(place, *slots, *pair, *before)


def field_kernel(freqs, order, place_ref, *refs):
    pieces, kernels, out_ref = refs[: len(order)], refs[len(order) : -1], refs[-1]
    own = place_ref[2]
    columns = pieces[0].shape[0]
    half = columns // 2
    field = out_ref.shape[0]
    wide = 2 * field
    products = [[None] * (len(kernels) // 2) for _ in range(2)]
    for k, piece in zip(order, pieces, strict=True):
        rows = pl.ds(pl.multiple_of((own ^ k) * PANEL_DEV, PANEL_DEV), PANEL_DEV)
        for part in range(2):
            for at, ref in enumerate(kernels):
                term = jnp.dot(piece[...], ref[part, rows, :], preferred_element_type=F32)
                before = products[part][at // 2]
                products[part][at // 2] = term if before is None else before + term
    row = lax.broadcasted_iota(jnp.int32, (columns, wide), 0)
    freq_of = (row % half) // (half // freqs)
    sums = []
    for part in range(2):
        blocks = [p[:, i : i + wide] for p in products[part] for i in range(0, p.shape[1], wide)]
        picked = blocks[0]
        for pair in range(1, freqs // 2):
            picked = jnp.where(freq_of // 2 == pair, blocks[pair], picked)
        sums.append(jnp.where(freq_of % 2 == 1, pltpu.roll(picked, field, 1), picked))
    real = sums[0][:half] - sums[1][half:]
    imag = sums[0][half:] + sums[1][:half]
    out_ref[...] = jnp.concatenate([real, imag], axis=0).T[:field]


def field_sums(freqs, field, place, pieces, kernels):
    columns = pieces[0].shape[0]
    vmem = pl.BlockSpec(memory_space=pltpu.VMEM)
    return pl.pallas_call(
        functools.partial(field_kernel, freqs, tuple(pieces)),
        in_specs=[pl.BlockSpec(memory_space=pltpu.SMEM)] + [vmem] * (len(pieces) + len(kernels)),
        out_specs=vmem,
        out_shape=jax.ShapeDtypeStruct((field, columns), F32),
        compiler_params=pltpu.CompilerParams(vmem_limit_bytes=24 * MIB),
        name="field_sums",
    )(place, *pieces.values(), *kernels)


def tree(terms):
    while len(terms) > 1:
        terms = [a + b for a, b in zip(terms[::2], terms[1::2], strict=True)]
    return terms[0]


def swap(x, axis, size, k):
    return lax.ppermute(x, axis, [(i, i ^ k) for i in range(size)])


def far_first(size):
    return range(size - 1, 0, -1)


def pack(x, shift):
    scaled = (x * jnp.exp2(shift)).astype(F16).reshape(-1, x.shape[-1])
    note = jnp.broadcast_to(shift.reshape(1, -1), (8, x.shape[-1])).astype(F16)
    return jnp.concatenate([scaled, note], axis=0)


def unpack(y, shape):
    shift = y[-8:-7].astype(F32).reshape(1, 1, 1, -1)
    return y[:-8].reshape(shape).astype(F32) * jnp.exp2(-shift), shift


def beside(x, work):
    return lax.optimization_barrier((x, work))


def shards(nodes_axis, field_axis):
    chips = nodes_axis // 2
    chip_bits = chips.bit_length() - 1

    def body(pressure, modes, omega_mode, damping, omega_force, panel_of, dist_bin):
        columns = pressure.shape[1]
        half = columns // 2
        width = modes.shape[1] // 2
        tiles = width // 128
        group = half // chips
        node = lax.axis_index("node")
        core, chip, fld = node % 2, node // 2, lax.axis_index("fld")
        place = jnp.stack([core, chip, fld]).astype(jnp.int32)

        away, away_top, left = forces_half(
            (1 - core).reshape(1), pressure.reshape(-1, row_block(pressure.shape[0]), columns), modes, True
        )
        came, came_top = (swap(x, "node", nodes_axis, 1) for x in (away, away_top))
        near = pltpu.with_memory_space_constraint(modes, pltpu.VMEM)
        home, home_top = forces_half(core.reshape(1), left, near, False)
        total = (home + came).reshape(tiles, 2, half, 128)
        bound = jnp.maximum(home_top[:1] + came_top[:1], 1e-30)
        shift = (14.0 - jnp.ceil(jnp.log2(bound))).reshape(1, 1, 1, 128)

        share = (tiles, 2, group, 128)
        sent = [
            pack(lax.dynamic_slice_in_dim(total, (chip ^ k) * group, group, 2), shift) for k in far_first(chips)
        ]
        sent, panel_known = beside(sent, panel_of)
        came = [swap(piece, "node", nodes_axis, 2 * k) for k, piece in zip(far_first(chips), sent, strict=True)]
        came, first = beside(came, panel_modes(core.reshape(1), panel_known, modes))
        terms, shifts = [], [shift]
        for piece in came:
            value, other = unpack(piece, share)
            terms.append(value)
            shifts.append(other)
        forces = tree(terms + [lax.dynamic_slice_in_dim(total, chip * group, group, 2)])
        shift = functools.reduce(jnp.minimum, shifts) - chip_bits

        freqs = omega_force.shape[0]
        bins, kernels = dist_bin.T, []
        for bit in range(field_axis.bit_length() - 1):
            packed, bins = beside(pack(forces, shift), bins)
            came = swap(packed, "fld", field_axis, 1 << bit)
            if bit < 2:
                came, kernel = beside(came, radiation(2 * bit, 2, omega_force, bins))
                kernels.extend(kernel)
            value, other = unpack(came, share)
            forces = forces + value
            shift = jnp.minimum(shift, other) - 1.0

        wmod = lax.dynamic_slice_in_dim(omega_mode, core * width, width).reshape(tiles, 1, 128)
        damp = lax.dynamic_slice_in_dim(damping, core * width, width).reshape(tiles, 1, 128)
        wcol = jnp.repeat(omega_force, half // omega_force.shape[0])
        wcol = lax.dynamic_slice_in_dim(wcol, chip * group, group)[None, :, None]
        real_part = wmod * wmod - wcol * wcol
        imag_part = 2.0 * damp * wmod * wcol
        magnitude = real_part * real_part + imag_part * imag_part
        h_real = real_part / magnitude
        h_imag = -imag_part / magnitude
        a_real = h_real * forces[:, 0] - h_imag * forces[:, 1]
        a_imag = h_real * forces[:, 1] + h_imag * forces[:, 0]
        response = jnp.stack([a_real, a_imag], axis=1).astype(BF16)

        response, panel_known = beside(response, panel_known)
        came = [swap(response, "node", nodes_axis, 2 * k) for k in far_first(chips)]
        came, second = beside(came, panel_modes((1 - core).reshape(1), panel_known, modes))
        sides = [[*came, response]]
        sides.append([swap(slot, "node", nodes_axis, 1) for slot in sides[0]])
        if group % 16:
            order = chips - 1 - (chip ^ jnp.arange(chips))
            sides = [
                [jnp.moveaxis(jnp.stack(side)[order], 0, 2).reshape(tiles, 2, half, 128)] for side in sides
            ]
        sums = panel_sums(place, sides[0], first)
        sums = panel_sums(place, sides[1], second, sums)
        sums, bins = beside(sums, bins)
        pieces = {k: swap(sums, "fld", field_axis, k) for k in (2, 3, 1)} | {0: sums}
        done = sum(x.shape[2] // dist_bin.shape[1] for x in kernels[::2])
        kernels.extend(radiation(done, freqs - done, omega_force, bins))
        field = field_sums(freqs, dist_bin.shape[1], place, pieces, kernels)
        field = field + swap(field, "node", nodes_axis, 1)
        return tree([swap(field, "node", nodes_axis, 2 * k) for k in far_first(chips)] + [field])

    return body


def solution(mesh):
    in_specs = (
        P(("node", "fld"), None),
        P(("node", "fld"), None),
        P(),
        P(),
        P(),
        P(("node", "fld")),
        P("node", "fld"),
    )
    out_specs = P("fld", None)
    body = shards(mesh.shape["node"], mesh.shape["fld"])
    return jax.shard_map(body, mesh=mesh, in_specs=in_specs, out_specs=out_specs, check_vma=False)
```

```python
import functools
import math

import jax
import jax.numpy as jnp
from jax import lax
from jax.experimental import pallas as pl
from jax.experimental.pallas import tpu as pltpu
from jax.sharding import PartitionSpec as P

PANEL_DEV = 256
BF16, F16, F32 = jnp.bfloat16, jnp.float16, jnp.float32
NT = (((1,), (1,)), ((), ()))
MIB = 1024 * 1024


def row_block(rows):
    return next(b for b in (256, 128, 64, 32, 16, rows) if rows % b == 0)


def start_rows(modes_ref, held_ref, sems, first):
    nodes, width = held_ref.shape
    rows = nodes // sems.shape[0]
    copies = []
    for k in range(sems.shape[0]):
        block = pl.ds(k * rows, rows)
        copies.append(
            pltpu.make_async_copy(
                modes_ref.at[block, pl.ds(first, width)], held_ref.at[block, :], sems.at[k]
            )
        )
        copies[-1].start()
    return rows, copies


def forces_sums(left_ref, block_of, copies, rows, out_ref, top_ref):
    for k in range(left_ref.shape[1] // rows):
        if copies:
            copies[k].wait()
        block = slice(k * rows, (k + 1) * rows)
        part = jnp.dot(left_ref[:, block], block_of(block), preferred_element_type=F32)
        for t in range(out_ref.shape[0]):
            tile = part[:, t * 128 : (t + 1) * 128]
            out_ref[t] = tile if k == 0 else out_ref[t] + tile
    top_ref[...] = jnp.full(top_ref.shape, jnp.max(jnp.abs(out_ref[...])), F32)


def first_kernel(half_ref, pressure_ref, modes_ref, out_ref, top_ref, left_ref, loads_ref, held_ref, sem, sems):
    load = pltpu.make_async_copy(pressure_ref, loads_ref, sem)
    load.start()
    width = held_ref.shape[1]
    rows, copies = start_rows(modes_ref, held_ref, sems, pl.multiple_of(half_ref[0] * width, 128))
    load.wait()
    for k in range(loads_ref.shape[0]):
        part = loads_ref.shape[1]
        left_ref[:, k * part : (k + 1) * part] = loads_ref[k].T
    forces_sums(left_ref, lambda block: held_ref[block, :], copies, rows, out_ref, top_ref)


def second_kernel(half_ref, left_ref, modes_ref, out_ref, top_ref):
    width = modes_ref.shape[1] // 2
    columns = pl.ds(pl.multiple_of(half_ref[0] * width, 128), width)
    forces_sums(left_ref, lambda block: modes_ref[block, columns], None, row_block(left_ref.shape[1]), out_ref, top_ref)


def forces_half(half, pressure, modes, first):
    columns, nodes = (pressure.shape[2], modes.shape[0]) if first else pressure.shape
    width = modes.shape[1] // 2
    vmem, hbm = pl.BlockSpec(memory_space=pltpu.VMEM), pl.BlockSpec(memory_space=pltpu.HBM)
    outs = [
        jax.ShapeDtypeStruct((width // 128, columns, 128), F32),
        jax.ShapeDtypeStruct((8, 128), F32),
        jax.ShapeDtypeStruct((columns, nodes), BF16),
    ][: 3 if first else 2]
    scratch = [
        pltpu.VMEM(pressure.shape, BF16),
        pltpu.VMEM((nodes, width), BF16),
        pltpu.SemaphoreType.DMA,
        pltpu.SemaphoreType.DMA((nodes // row_block(nodes),)),
    ]
    if first:
        pressure, modes = (pltpu.with_memory_space_constraint(x, pltpu.HBM) for x in (pressure, modes))
    return pl.pallas_call(
        first_kernel if first else second_kernel,
        in_specs=[pl.BlockSpec(memory_space=pltpu.SMEM)] + ([hbm, hbm] if first else [vmem, vmem]),
        out_specs=[vmem] * len(outs),
        out_shape=outs,
        scratch_shapes=scratch if first else [],
        compiler_params=pltpu.CompilerParams(vmem_limit_bytes=16 * MIB),
        cost_estimate=pl.CostEstimate(
            flops=2 * nodes * columns * width, bytes_accessed=2 * nodes * width, transcendentals=0
        ),
        name="forces_half",
    )(half, pressure, modes)


def panel_modes_kernel(half_ref, panel_ref, modes_ref, high_ref, low_ref, onehot_ref, held_ref, total_ref, sems):
    width = held_ref.shape[1]
    rows, copies = start_rows(modes_ref, held_ref, sems, pl.multiple_of(half_ref[0] * width, 128))
    panels = lax.broadcasted_iota(jnp.int32, onehot_ref.shape, 0)
    onehot_ref[...] = jnp.where(panels == panel_ref[...], 1.0, 0.0).astype(BF16)
    for k, copy in enumerate(copies):
        copy.wait()
        block = slice(k * rows, (k + 1) * rows)
        part = jnp.dot(onehot_ref[:, block], held_ref[block, :], preferred_element_type=F32)
        total_ref[...] = part if k == 0 else total_ref[...] + part
    total = total_ref[...]
    high = total.astype(BF16)
    high_ref[...] = high
    low_ref[...] = (total - high.astype(F32)).astype(BF16)


def panel_modes(half, panel_of, modes):
    nodes, count = modes.shape
    width = count // 2
    blocks = 4 if nodes % 64 == 0 else 1
    return pl.pallas_call(
        panel_modes_kernel,
        in_specs=[
            pl.BlockSpec(memory_space=pltpu.SMEM),
            pl.BlockSpec(memory_space=pltpu.VMEM),
            pl.BlockSpec(memory_space=pltpu.HBM),
        ],
        out_specs=[pl.BlockSpec(memory_space=pltpu.VMEM)] * 2,
        out_shape=[jax.ShapeDtypeStruct((PANEL_DEV, width), BF16)] * 2,
        scratch_shapes=[
            pltpu.VMEM((PANEL_DEV, nodes), BF16),
            pltpu.VMEM((nodes, width), BF16),
            pltpu.VMEM((PANEL_DEV, width), F32),
            pltpu.SemaphoreType.DMA((blocks,)),
        ],
        compiler_params=pltpu.CompilerParams(vmem_limit_bytes=16 * MIB),
        cost_estimate=pl.CostEstimate(
            flops=2 * nodes * PANEL_DEV * width, bytes_accessed=2 * nodes * width, transcendentals=0
        ),
        name="panel_modes",
    )(half, panel_of.reshape(1, nodes), pltpu.with_memory_space_constraint(modes, pltpu.HBM))


def sin_cos(angle):
    turns = jnp.floor(angle * (2.0 / math.pi) + 0.5)
    rest = angle - turns * 1.5703125
    rest = rest - turns * 4.837512969970703125e-4
    rest = rest - turns * 7.549789948768648e-8
    square = rest * rest
    sine = rest + rest * square * (
        -1.6666654611e-1 + square * (8.3321608736e-3 - square * 1.9515295891e-4)
    )
    cosine = (1.0 - 0.5 * square) + square * square * (
        4.166664568298827e-2 + square * (-1.388731625493765e-3 + square * 2.443315711809948e-5)
    )
    quadrant = turns.astype(jnp.int32)
    swap = (quadrant & 1) == 1
    sin_sign = jnp.where((quadrant & 2) == 2, -1.0, 1.0)
    cos_sign = jnp.where(((quadrant + 1) & 2) == 2, -1.0, 1.0)
    return jnp.where(swap, cosine, sine) * sin_sign, jnp.where(swap, sine, cosine) * cos_sign


def radiation_kernel(first, omega_ref, bins_ref, high_ref, low_ref, dist_ref):
    pair = pl.program_id(0)

    @pl.when(pair == 0)
    def _():
        dist = 1.0 + 0.05 * bins_ref[...].astype(F32)
        dist_ref[...] = jnp.concatenate([dist, dist], axis=0).T

    dist = dist_ref[...]
    lane = lax.broadcasted_iota(jnp.int32, (1, dist.shape[1]), 1)
    freq = first + 2 * pair
    omega = jnp.where(lane < dist.shape[1] // 2, omega_ref[freq], omega_ref[freq + 1])
    sine, cosine = sin_cos(omega * dist)
    gain = (-0.01 / (2.0 * math.pi)) * omega * omega / dist
    for part, value in enumerate((gain * cosine, -gain * sine)):
        high = value.astype(BF16)
        high_ref[part] = high
        low_ref[part] = (value - high.astype(F32)).astype(BF16)


def radiation(first, count, omega_force, bins):
    field, panels = bins.shape
    return pl.pallas_call(
        functools.partial(radiation_kernel, first),
        grid=(count // 2,),
        in_specs=[
            pl.BlockSpec(memory_space=pltpu.SMEM),
            pl.BlockSpec((field, panels), lambda q: (0, 0)),
        ],
        out_specs=[pl.BlockSpec((2, panels, 2 * field), lambda q: (0, 0, q))] * 2,
        out_shape=[jax.ShapeDtypeStruct((2, panels, count * field), BF16)] * 2,
        scratch_shapes=[pltpu.VMEM((panels, 2 * field), F32)],
        compiler_params=pltpu.CompilerParams(vmem_limit_bytes=16 * MIB),
        cost_estimate=pl.CostEstimate(
            flops=40 * count * field * panels, bytes_accessed=4 * count * field * panels, transcendentals=0
        ),
        name="radiation",
    )(omega_force, bins)


def panel_sums_kernel(count, place_ref, *refs):
    slots, (high_ref, low_ref), before, (out_ref, held_ref) = refs[:count], refs[count : count + 2], refs[count + 2 : -2], refs[-2:]
    chip = place_ref[1]
    tiles, _, group, lanes = slots[0].shape
    half = held_ref.shape[0] // 2
    for k, slot in enumerate(slots):
        start = 0 if count == 1 else pl.multiple_of((chip ^ (count - 1 - k)) * group, group)
        for part in range(2):
            for t in range(tiles):
                held_ref[pl.ds(part * half + start, group), t * lanes : (t + 1) * lanes] = slot[t, part]
    total = before[0][...] if before else None
    for ref in (high_ref, low_ref):
        term = lax.dot_general(held_ref[...], ref[...], NT, preferred_element_type=F32)
        total = term if total is None else total + term
    out_ref[...] = total.astype(out_ref.dtype)


def panel_sums(place, slots, pair, *before):
    half = slots[0].shape[2] * len(slots)
    width = slots[0].shape[0] * slots[0].shape[3]
    vmem = pl.BlockSpec(memory_space=pltpu.VMEM)
    return pl.pallas_call(
        functools.partial(panel_sums_kernel, len(slots)),
        in_specs=[pl.BlockSpec(memory_space=pltpu.SMEM)] + [vmem] * (len(slots) + 2 + len(before)),
        out_specs=vmem,
        out_shape=jax.ShapeDtypeStruct((2 * half, PANEL_DEV), BF16 if before else F32),
        scratch_shapes=[pltpu.VMEM((2 * half, width), BF16)],
        compiler_params=pltpu.CompilerParams(vmem_limit_bytes=16 * MIB),
        cost_estimate=pl.CostEstimate(
            flops=8 * half * width * PANEL_DEV, bytes_accessed=8 * width * PANEL_DEV, transcendentals=0
        ),
        name="panel_sums",
    )(place, *slots, *pair, *before)


def field_products(order, own, pieces, kernels, before):
    products = []
    for part in range(2):
        blocks, at = [], 0
        for high, low in zip(kernels[::2], kernels[1::2], strict=True):
            width = high.shape[2]
            total = before[part, :, at : at + width] if before is not None else None
            for k, piece in zip(order, pieces, strict=True):
                rows = pl.ds(pl.multiple_of((own ^ k) * PANEL_DEV, PANEL_DEV), PANEL_DEV)
                for ref in (high, low):
                    term = jnp.dot(piece[...], ref[part, rows, :], preferred_element_type=F32)
                    total = term if total is None else total + term
            blocks.append(total)
            at += width
        products.append(blocks)
    return products


def field_start_kernel(order, place_ref, *refs):
    pieces, kernels, out_ref = refs[: len(order)], refs[len(order) : -1], refs[-1]
    for part, blocks in enumerate(field_products(order, place_ref[2], pieces, kernels, None)):
        at = 0
        for block in blocks:
            out_ref[part, :, at : at + block.shape[1]] = block
            at += block.shape[1]


def field_kernel(freqs, order, place_ref, *refs):
    pieces, (*kernels, before_ref, out_ref) = refs[: len(order)], refs[len(order) :]
    columns = pieces[0].shape[0]
    half = columns // 2
    field = out_ref.shape[0]
    wide = 2 * field
    row = lax.broadcasted_iota(jnp.int32, (columns, wide), 0)
    freq_of = (row % half) // (half // freqs)
    sums = []
    for products in field_products(order, place_ref[2], pieces, kernels, before_ref):
        blocks = [p[:, i : i + wide] for p in products for i in range(0, p.shape[1], wide)]
        picked = blocks[0]
        for pair in range(1, freqs // 2):
            picked = jnp.where(freq_of // 2 == pair, blocks[pair], picked)
        sums.append(jnp.where(freq_of % 2 == 1, pltpu.roll(picked, field, 1), picked))
    real = sums[0][:half] - sums[1][half:]
    imag = sums[0][half:] + sums[1][:half]
    out_ref[...] = jnp.concatenate([real, imag], axis=0).T[:field]


def field_sums(freqs, field, place, pieces, kernels, *before):
    columns = next(iter(pieces.values())).shape[0]
    vmem = pl.BlockSpec(memory_space=pltpu.VMEM)
    order = tuple(pieces)
    return pl.pallas_call(
        functools.partial(field_kernel, freqs, order) if before else functools.partial(field_start_kernel, order),
        in_specs=[pl.BlockSpec(memory_space=pltpu.SMEM)] + [vmem] * (len(pieces) + len(kernels) + len(before)),
        out_specs=vmem,
        out_shape=jax.ShapeDtypeStruct((field, columns) if before else (2, columns, freqs * field), F32),
        compiler_params=pltpu.CompilerParams(vmem_limit_bytes=24 * MIB),
        name="field_sums",
    )(place, *pieces.values(), *kernels, *before)


def tree(terms):
    while len(terms) > 1:
        terms = [a + b for a, b in zip(terms[::2], terms[1::2], strict=True)]
    return terms[0]


def swap(x, axis, size, k):
    return lax.ppermute(x, axis, [(i, i ^ k) for i in range(size)])


def far_first(size):
    return range(size - 1, 0, -1)


def pack(x, shift):
    scaled = (x * jnp.exp2(shift)).astype(F16).reshape(-1, x.shape[-1])
    note = jnp.broadcast_to(shift.reshape(1, -1), (8, x.shape[-1])).astype(F16)
    return jnp.concatenate([scaled, note], axis=0)


def unpack(y, shape):
    shift = y[-8:-7].astype(F32).reshape(1, 1, 1, -1)
    return y[:-8].reshape(shape).astype(F32) * jnp.exp2(-shift), shift


def beside(x, work):
    return lax.optimization_barrier((x, work))


def shards(nodes_axis, field_axis):
    chips = nodes_axis // 2
    chip_bits = chips.bit_length() - 1

    def body(pressure, modes, omega_mode, damping, omega_force, panel_of, dist_bin):
        columns = pressure.shape[1]
        half = columns // 2
        width = modes.shape[1] // 2
        tiles = width // 128
        group = half // chips
        node = lax.axis_index("node")
        core, chip, fld = node % 2, node // 2, lax.axis_index("fld")
        place = jnp.stack([core, chip, fld]).astype(jnp.int32)

        away, away_top, left = forces_half(
            (1 - core).reshape(1), pressure.reshape(-1, row_block(pressure.shape[0]), columns), modes, True
        )
        came, came_top = (swap(x, "node", nodes_axis, 1) for x in (away, away_top))
        near = pltpu.with_memory_space_constraint(modes, pltpu.VMEM)
        home, home_top = forces_half(core.reshape(1), left, near, False)
        total = (home + came).reshape(tiles, 2, half, 128)
        bound = jnp.maximum(home_top[:1] + came_top[:1], 1e-30)
        shift = (14.0 - jnp.ceil(jnp.log2(bound))).reshape(1, 1, 1, 128)

        share = (tiles, 2, group, 128)
        sent = [
            pack(lax.dynamic_slice_in_dim(total, (chip ^ k) * group, group, 2), shift) for k in far_first(chips)
        ]
        sent, panel_known, omega_known = lax.optimization_barrier((sent, panel_of, omega_force))
        came = [swap(piece, "node", nodes_axis, 2 * k) for k, piece in zip(far_first(chips), sent, strict=True)]
        came, first = beside(came, panel_modes(core.reshape(1), panel_known, modes))
        terms, shifts = [], [shift]
        for piece in came:
            value, other = unpack(piece, share)
            terms.append(value)
            shifts.append(other)
        forces = tree(terms + [lax.dynamic_slice_in_dim(total, chip * group, group, 2)])
        shift = functools.reduce(jnp.minimum, shifts) - chip_bits

        freqs = omega_force.shape[0]
        bins, kernels = dist_bin.T, []
        for bit in range(field_axis.bit_length() - 1):
            packed, bins = beside(pack(forces, shift), bins)
            came = swap(packed, "fld", field_axis, 1 << bit)
            if bit < 2:
                came, kernel = beside(came, radiation(2 * bit, 2, omega_force, bins))
                kernels.extend(kernel)
            value, other = unpack(came, share)
            forces = forces + value
            shift = jnp.minimum(shift, other) - 1.0

        wmod = lax.dynamic_slice_in_dim(omega_mode, core * width, width).reshape(tiles, 1, 128)
        damp = lax.dynamic_slice_in_dim(damping, core * width, width).reshape(tiles, 1, 128)
        wcol = jnp.repeat(omega_known, half // omega_force.shape[0])
        wcol = lax.dynamic_slice_in_dim(wcol, chip * group, group)[None, :, None]
        real_part = wmod * wmod - wcol * wcol
        imag_part = 2.0 * damp * wmod * wcol
        magnitude = real_part * real_part + imag_part * imag_part
        h_real = real_part / magnitude
        h_imag = -imag_part / magnitude
        a_real = h_real * forces[:, 0] - h_imag * forces[:, 1]
        a_imag = h_real * forces[:, 1] + h_imag * forces[:, 0]
        response = jnp.stack([a_real, a_imag], axis=1).astype(BF16)

        response, panel_known = beside(response, panel_known)
        came = [swap(response, "node", nodes_axis, 2 * k) for k in far_first(chips)]
        came, second = beside(came, panel_modes((1 - core).reshape(1), panel_known, modes))
        sides = [[*came, response]]
        sides.append([swap(slot, "node", nodes_axis, 1) for slot in sides[0]])
        if group % 16:
            order = chips - 1 - (chip ^ jnp.arange(chips))
            sides = [
                [jnp.moveaxis(jnp.stack(side)[order], 0, 2).reshape(tiles, 2, half, 128)] for side in sides
            ]
        sums = panel_sums(place, sides[0], first)
        sums = panel_sums(place, sides[1], second, sums)
        sums, bins = beside(sums, bins)
        pieces = {k: swap(sums, "fld", field_axis, k) for k in (2, 3, 1)} | {0: sums}
        done = sum(x.shape[2] // dist_bin.shape[1] for x in kernels[::2])
        kernels.extend(radiation(done, freqs - done, omega_force, bins))
        arrived = {k: pieces[k] for k in (0, field_axis // 2)}
        waited = {k: piece for k, piece in pieces.items() if k not in arrived}
        sizes = (freqs, dist_bin.shape[1], place)
        field = field_sums(*sizes, waited, kernels, field_sums(*sizes, arrived, kernels))
        field = field + swap(field, "node", nodes_axis, 1)
        return tree([swap(field, "node", nodes_axis, 2 * k) for k in far_first(chips)] + [field])

    return body


def solution(mesh):
    in_specs = (
        P(("node", "fld"), None),
        P(("node", "fld"), None),
        P(),
        P(),
        P(),
        P(("node", "fld")),
        P("node", "fld"),
    )
    out_specs = P("fld", None)
    body = shards(mesh.shape["node"], mesh.shape["fld"])
    return jax.shard_map(body, mesh=mesh, in_specs=in_specs, out_specs=out_specs, check_vma=False)
```
